32 devices in a mesh: dp: 8 (over z, y), seq: 4 (over x, core).
Axes of the slice: x: 2, y: 2, z: 4, core: 2. Of those that a mesh axis runs over, the one named last changes fastest.
Arguments:
- inputs: bfloat16 [8, 1536, 1024], P('dp', 'seq'), may hold values from -6 to 6
- conv_weight: bfloat16 [1024, 3, 384], P(('dp', 'seq')), may hold values from -0.109375 to 0.109375
- out_weight: bfloat16 [1024, 384], P(('dp', 'seq')), may hold values from -0.3125 to 0.3125
- cotangent: bfloat16 [8, 1536, 1024], P('dp', 'seq'), may hold values from -8 to 8
Outputs:
- outputs: bfloat16 [8, 1536, 1024], P('dp', 'seq')
- input_grad: bfloat16 [8, 1536, 1024], P('dp', 'seq')
- conv_grad: float32 [1024, 3, 384], P(('dp', 'seq'))
- out_grad: float32 [1024, 384], P(('dp', 'seq'))
The draws below stay inside these ranges and needn't reach their ends.
All inputs are finite; a program needn't handle non-finite values.
Results may differ from the reference program's by a relative error of at most 0.009.
Values may be sent and summed in bfloat16 or wider, within the bound.
A program may use at most 64 MiB of HBM per device.

```python
import jax
import jax.numpy as jnp
from jax import lax

C = 1024
HIDDEN_CHANNELS = 384
DILATION_STEP = 192
WINDOW_LENGTH = 1536
BATCH = 8


def with_spikes(values, key, source, target, blocks, factor):
    def block_of(dim):
        return (jnp.arange(values.shape[dim]) // (values.shape[dim] // blocks)).reshape((-1,) + (1,) * (values.ndim - 1 - dim))

    first = jax.random.permutation(key, blocks)[block_of(target)]
    second = (block_of(target) + blocks // 2) % blocks
    return jnp.where((block_of(source) == first) | (block_of(source) == second), factor * values, values)


def levels(stream_key, shape, cuts, least, largest):
    gain = 1.0
    for position, shards_of in cuts:
        steps = jax.random.uniform(jax.random.fold_in(jax.random.fold_in(stream_key, 6), position), (shards_of,), jnp.float32, least / len(cuts), largest / len(cuts))
        gain = gain * jnp.repeat(jnp.exp(steps), shape[position] // shards_of).reshape((-1,) + (1,) * (len(shape) - 1 - position))
    return gain


def centred(key, extent, width, limit, shards=(), dtype=jnp.bfloat16):
    drawn = width * jax.random.normal(key, extent, jnp.float32)
    if shards:
        drawn = drawn * levels(key, extent, shards, -0.22, 0.18)
    return jnp.clip(drawn, -limit, limit).astype(dtype)


def gaussian_with(own_key, extent, spread, limit, pieces, heavy, kind=jnp.bfloat16):
    result = spread * jax.random.normal(own_key, extent, jnp.float32)
    if pieces:
        result = result * levels(own_key, extent, pieces, -0.22, 0.18)
    return jnp.clip(with_spikes(result, jax.random.fold_in(own_key, 3), *heavy), -limit, limit).astype(kind)


def setup_inputs(seed: int = 0) -> dict:
    key_list = jax.random.split(jax.random.key(seed), 5)
    return {
        "inputs": centred(key_list[0], (BATCH, WINDOW_LENGTH, C), 1.0, 6.0, ((0, 8), (1, 4))),
        "conv_weight": centred(key_list[1], (C, 3, HIDDEN_CHANNELS), (3 * C) ** -0.5, 0.109375, ((0, 32),)),
        "out_weight": centred(key_list[2], (C, HIDDEN_CHANNELS), HIDDEN_CHANNELS ** -0.5, 0.3125, ((0, 32),)),
        "cotangent": gaussian_with(key_list[3], (BATCH, WINDOW_LENGTH, C), 1.0, 8.0, ((0, 8), (1, 4)), (0, 2, 8, 2.0)),
    }


def window_pass(inputs, cotangent, conv_weight, out_weight):
    wflat = conv_weight.reshape(C, 3 * HIDDEN_CHANNELS)
    activated_value = jax.nn.gelu(inputs.astype(jnp.float32)).astype(jnp.bfloat16)
    prod = jnp.dot(activated_value, wflat, preferred_element_type=jnp.float32).astype(jnp.bfloat16)
    opening_slice = prod[:, :HIDDEN_CHANNELS]
    middle = prod[:, HIDDEN_CHANNELS:2 * HIDDEN_CHANNELS]
    closing_slice = prod[:, 2 * HIDDEN_CHANNELS:]
    empty_columns = jnp.zeros((DILATION_STEP, HIDDEN_CHANNELS), jnp.bfloat16)
    leading_part = jnp.concatenate([empty_columns, opening_slice[:WINDOW_LENGTH - DILATION_STEP]], axis=0)
    trailing_part = jnp.concatenate([closing_slice[DILATION_STEP:], empty_columns], axis=0)
    pre = leading_part.astype(jnp.float32) + middle.astype(jnp.float32) + trailing_part.astype(jnp.float32)
    mid = jax.nn.gelu(pre).astype(jnp.bfloat16)
    outputs = (inputs.astype(jnp.float32) + jnp.dot(mid, out_weight.T, preferred_element_type=jnp.float32)).astype(jnp.bfloat16)
    dmid = jnp.dot(cotangent, out_weight, preferred_element_type=jnp.float32)
    preactivation_gradient = jax.vjp(jax.nn.gelu, pre)[1](dmid)[0].astype(jnp.bfloat16)
    zero_bordered = jnp.concatenate([empty_columns, preactivation_gradient, empty_columns], axis=0)
    offset_input = jnp.concatenate([zero_bordered[2 * DILATION_STEP:2 * DILATION_STEP + WINDOW_LENGTH], zero_bordered[DILATION_STEP:DILATION_STEP + WINDOW_LENGTH], zero_bordered[:WINDOW_LENGTH]], axis=1)
    dact = jnp.dot(offset_input, wflat.T, preferred_element_type=jnp.float32)
    conv_part = jnp.einsum('pc,pk->ck', activated_value, offset_input, preferred_element_type=jnp.float32)
    out_part = jnp.einsum('pc,ph->ch', cotangent, mid, preferred_element_type=jnp.float32)
    input_grad = (cotangent.astype(jnp.float32) + jax.vjp(jax.nn.gelu, inputs.astype(jnp.float32))[1](dact)[0]).astype(jnp.bfloat16)
    return (outputs, input_grad, conv_part, out_part)

def reference(inputs, conv_weight, out_weight, cotangent):

    def advance(carry, pair):
        outputs, input_grad, conv_part, out_part = window_pass(pair[0], pair[1], conv_weight, out_weight)
        return ((carry[0] + conv_part, carry[1] + out_part), (outputs, input_grad))
    start = (jnp.zeros((C, 3 * HIDDEN_CHANNELS), jnp.float32), jnp.zeros((C, HIDDEN_CHANNELS), jnp.float32))
    totals, results = lax.scan(advance, start, (inputs, cotangent))
    factor = 1.0 / jnp.sqrt(jnp.float32(BATCH * WINDOW_LENGTH))
    conv_grad = (totals[0] * factor).reshape(C, 3, HIDDEN_CHANNELS)
    out_grad = totals[1] * factor
    return (results[0], results[1], conv_grad, out_grad)
```

```python
import functools
import math

import jax
import jax.numpy as jnp
from jax import lax
from jax.experimental import pallas as pl
from jax.experimental.pallas import tpu as pltpu
from jax.sharding import PartitionSpec as P

F32 = jnp.float32
BF16 = jnp.bfloat16
ALPHA = math.sqrt(2.0 / math.pi)
BETA = 0.044715


def gelu_and_slope(x):
    x2 = x * x
    t = jnp.tanh(ALPHA * x * (1.0 + BETA * x2))
    half = 0.5 * (1.0 + t)
    slope = half + 0.5 * x * (1.0 - t * t) * (ALPHA * (1.0 + 3.0 * BETA * x2))
    return x * half, slope


def gelu_only(x):
    t = jnp.tanh(ALPHA * x * (1.0 + BETA * (x * x)))
    return x * (0.5 * (1.0 + t))


def block_kernel(
    planes, factor,
    in_ref, cot_ref, w_ref,
    out_ref, ig_ref, cg_ref,
    gat, xh, act, acc, mid, dpre, dacc, part, s0, s1a, s1b, s2,
    sb0, rb0, sb1a, rb1a, sb1b, rb1b, sb2a, rb2a, sb2b, rb2b, sb3, rb3,
    gz, gax, gay, gbx, gby, gc, hx, hd, q0, q1a, q1b, q2a, q2b, q3, qloc,
):
    dp = lax.axis_index("dp")
    seq = lax.axis_index("seq")
    z, y = dp // 2, dp % 2
    x, c = seq // 2, seq % 2
    oy, ox, oc = 1 - y, 1 - x, 1 - c
    rows, chans = in_ref.shape
    gap = rows // 2
    cz = chans // planes
    hidden = w_ref.shape[2]
    seqs = 4
    ypeer = (z * 2 + oy, seq)
    xpeer = (dp, ox * 2 + c)
    cpeer = (dp, x * 2 + oc)
    diag = (dp, ox * 2 + oc)

    def zpeer(d):
        return (lax.rem(z + d, planes) * 2 + y, seq)

    def copy(src, dst, sems, peer):
        return pltpu.make_async_remote_copy(
            src_ref=src, dst_ref=dst, send_sem=sems[0], recv_sem=sems[1],
            device_id=peer, device_id_type=pl.DeviceIdType.MESH,
        )

    def pair(sem, *index):
        return sem.at[(0,) + index], sem.at[(1,) + index]

    def columns(i):
        return pl.ds(pl.multiple_of(i * cz, cz), cz)

    barrier = pltpu.get_barrier_semaphore()
    peers = [ypeer, xpeer, cpeer, diag] + [zpeer(d) for d in range(1, planes)]
    own = gat.at[:, z, y, x, c]
    mine = pltpu.make_async_copy(w_ref, own, qloc)
    mine.start()
    for peer in peers:
        pl.semaphore_signal(barrier, inc=1, device_id=peer, device_id_type=pl.DeviceIdType.MESH)
    mine.wait()
    pl.semaphore_wait(barrier, len(peers))

    sends = []

    def go(*copies):
        for one in copies:
            one.start()
            sends.append(one)
        return copies

    def arrived(copies):
        for one in copies:
            one.wait_recv()

    def at(d):
        return lax.rem(z + planes - d, planes)

    zs = [None] + [
        go(copy(own, own, pair(gz, d - 1), zpeer(d)))
        for d in range(1, planes)
    ]

    def spread(d):
        i = at(d)
        a = gat.at[0:2, i, y, x, c]
        b = gat.at[2:4, i, y, x, c]
        links = go(copy(a, a, pair(gay, d), ypeer), copy(b, b, pair(gax, d), xpeer))
        whole = gat.at[:, i, y, x, c]
        return links, go(copy(whole, whole, pair(gc, d, 0), cpeer))

    def spread_again(d):
        i = at(d)
        a = gat.at[0:2, i, :, x, c]
        b = gat.at[2:4, i, y, :, c]
        links = go(copy(a, a, pair(gbx, d), xpeer), copy(b, b, pair(gby, d), ypeer))
        a = gat.at[0:2, i, oy, x, c]
        b = gat.at[2:4, i, y, ox, c]
        return links, go(copy(a, a, pair(gc, d, 1), cpeer), copy(b, b, pair(gc, d, 2), cpeer))

    def share(d):
        i = at(d)
        a = gat.at[0:2, i, :, ox, c]
        b = gat.at[2:4, i, oy, :, c]
        return go(copy(a, a, pair(gc, d, 3), cpeer), copy(b, b, pair(gc, d, 4), cpeer))

    def neighbours(lower, upper, left, right, sem):
        to_right = copy(upper, left, pair(sem, 0), (dp, lax.rem(seq + 1, seqs)))
        to_left = copy(lower, right, pair(sem, 1), (dp, lax.rem(seq + seqs - 1, seqs)))
        return to_right, to_left

    def start_halo(halo):
        pl.when(seq < seqs - 1)(halo[0].start)
        pl.when(seq > 0)(halo[1].start)

    def wait_halo(halo):
        pl.when(seq > 0)(halo[0].wait_recv)
        pl.when(seq < seqs - 1)(halo[1].wait_recv)

    def wait_halo_sends(halo):
        pl.when(seq < seqs - 1)(halo[0].wait_send)
        pl.when(seq > 0)(halo[1].wait_send)

    tile = 32

    def activate_own():
        @pl.loop(0, rows // tile)
        def _(r):
            at_row = pl.multiple_of(r * tile, tile)
            value = in_ref[pl.ds(at_row, tile), :].astype(F32)
            act[pl.ds(pl.multiple_of(gap + at_row, tile), tile), :] = gelu_only(value).astype(BF16)

    def activate_halo():
        for side, start in ((0, 0), (1, gap + rows)):
            inside = (seq > 0) if side == 0 else (seq < seqs - 1)

            @pl.when(inside)
            def _():
                @pl.loop(0, gap // tile)
                def _(r):
                    at_row = pl.multiple_of(r * tile, tile)
                    value = xh[side, pl.ds(at_row, tile), :].astype(F32)
                    act[pl.ds(pl.multiple_of(start + at_row, tile), tile), :] = gelu_only(value).astype(BF16)

            @pl.when(jnp.logical_not(inside))
            def _():
                act[start:start + gap, :] = jnp.zeros((gap, chans), BF16)
                dpre[start:start + gap, :] = jnp.zeros((gap, hidden), BF16)

    def weight(k, i):
        return gat[k, i].reshape(cz, hidden)

    def multiply(d):
        i = at(d)
        for k in range(4):
            left = act[k * gap:k * gap + rows, columns(i)] if k < 3 else cot_ref[:, columns(i)]
            value = jnp.dot(left, weight(k, i), preferred_element_type=F32)
            if d == 0:
                acc[k] = value
            else:
                acc[k] += value

    first, second, cores = {}, {}, {}
    halo = neighbours(in_ref.at[0:gap], in_ref.at[gap:rows], xh.at[0], xh.at[1], hx)
    for t in range(planes + 3):
        if t < planes:
            if t > 0:
                arrived(zs[t])
            first[t], cores[t] = spread(t)
        if t == 0:
            start_halo(halo)
            activate_own()
        if 0 <= t - 1 < planes:
            arrived(first[t - 1])
            second[t - 1], more = spread_again(t - 1)
            cores[t - 1] += more
        if 0 <= t - 2 < planes:
            arrived(second[t - 2])
            cores[t - 2] += share(t - 2)
        if t == 3:
            wait_halo(halo)
            activate_halo()
        if 0 <= t - 3 < planes:
            arrived(cores[t - 3])
            multiply(t - 3)

    @pl.loop(0, rows // tile)
    def _(r):
        here = pl.ds(pl.multiple_of(r * tile, tile), tile)
        pre = acc[0, here, :].astype(BF16).astype(F32)
        pre += acc[1, here, :].astype(BF16).astype(F32)
        pre += acc[2, here, :].astype(BF16).astype(F32)
        value, slope = gelu_and_slope(pre)
        mid[here, :] = value.astype(BF16)
        dpre[pl.ds(pl.multiple_of(gap + r * tile, tile), tile), :] = (acc[3, here, :] * slope).astype(BF16)

    halo_d = neighbours(
        dpre.at[gap:2 * gap], dpre.at[2 * gap:3 * gap],
        dpre.at[0:gap], dpre.at[gap + rows:2 * gap + rows], hd,
    )
    start_halo(halo_d)

    def to(d):
        return lax.rem(z + d, planes)

    def partial(n, d):
        for k in range(4):
            if k < 3:
                left, right = act[k * gap:k * gap + rows, columns(to(d))], dpre[gap:gap + rows, :]
            else:
                left, right = cot_ref[:, columns(to(d))], mid[...]
            value = lax.dot_general(left, right, (((0,), (0,)), ((), ())), preferred_element_type=F32)
            part[n % 2, k] = value.reshape(part.shape[2:])
        sb0[n] = part[n % 2, :, :, :, oc].astype(BF16)
        return go(copy(sb0.at[n], rb0.at[n], pair(q0, n), cpeer))

    def sum_cores(n, copies):
        arrived(copies)
        s0[n % 2] = part[n % 2, :, :, :, c] + rb0[n].astype(F32)
        sb1a[n] = s0[n % 2, 0:2, :, ox].astype(BF16)
        sb1b[n] = s0[n % 2, 2:4, oy].astype(BF16)
        return go(
            copy(sb1a.at[n], rb1a.at[n], pair(q1a, n), xpeer),
            copy(sb1b.at[n], rb1b.at[n], pair(q1b, n), ypeer),
        )

    def sum_first(n, copies):
        arrived(copies)
        s1a[n % 2] = s0[n % 2, 0:2, :, x] + rb1a[n].astype(F32)
        s1b[n % 2] = s0[n % 2, 2:4, y] + rb1b[n].astype(F32)
        sb2a[n] = s1a[n % 2, :, oy].astype(BF16)
        sb2b[n] = s1b[n % 2, :, ox].astype(BF16)
        return go(
            copy(sb2a.at[n], rb2a.at[n], pair(q2a, n), ypeer),
            copy(sb2b.at[n], rb2b.at[n], pair(q2b, n), xpeer),
        )

    def sum_second(n, d, copies):
        arrived(copies)
        s2[0:2] = s1a[n % 2, :, y] + rb2a[n].astype(F32)
        s2[2:4] = s1b[n % 2, :, x] + rb2b[n].astype(F32)
        if d == 0:
            return ()
        sb3[n] = s2[...].astype(BF16)
        return go(copy(sb3.at[n], rb3.at[n], pair(q3, n), zpeer(d)))

    def finish_columns(j):
        here = slice(j * cz, (j + 1) * cz)
        nt = (((1,), (1,)), ((), ()))
        total = lax.dot_general(dpre[2 * gap:4 * gap, :], weight(0, j), nt, preferred_element_type=F32)
        total += lax.dot_general(dpre[gap:3 * gap, :], weight(1, j), nt, preferred_element_type=F32)
        total += lax.dot_general(dpre[0:2 * gap, :], weight(2, j), nt, preferred_element_type=F32)
        dacc[0] = total
        dacc[1] = lax.dot_general(mid[...], weight(3, j), nt, preferred_element_type=F32)

        @pl.loop(0, rows // tile)
        def _(r):
            at_row = pl.ds(pl.multiple_of(r * tile, tile), tile)
            source = in_ref[at_row, here].astype(F32)
            out_ref[at_row, here] = (source + dacc[1, at_row, :]).astype(BF16)
            slope = gelu_and_slope(source)[1]
            ig_ref[at_row, here] = (cot_ref[at_row, here].astype(F32) + dacc[0, at_row, :] * slope).astype(BF16)

    order = list(range(1, planes)) + [0]
    r0, r1, r2, r3 = {}, {}, {}, []
    fills = list(range(planes))
    for t in range(planes + 3):
        if 0 <= t - 3 < planes:
            r3 += sum_second(t - 3, order[t - 3], r2[t - 3])
        if 0 <= t - 2 < planes:
            r2[t - 2] = sum_first(t - 2, r1[t - 2])
        if 0 <= t - 1 < planes:
            r1[t - 1] = sum_cores(t - 1, r0[t - 1])
        if t < planes:
            r0[t] = partial(t, order[t])
        if t >= 2 and fills:
            if t == 2:
                wait_halo(halo_d)
            finish_columns(fills.pop(0))
    for j in fills:
        finish_columns(j)
    arrived(r3)
    total = s2[...]
    for n in range(planes - 1):
        total += rb3[n].astype(F32)
    cg_ref[...] = total * factor

    for one in sends:
        one.wait_send()
    wait_halo_sends(halo)
    wait_halo_sends(halo_d)


def fused(planes, inputs, conv_weight, out_weight, cotangent):
    rows, chans = inputs.shape[1:]
    share, taps, hidden = conv_weight.shape
    factor = 1.0 / math.sqrt(rows * lax.axis_size("seq") * lax.axis_size("dp"))
    w = jnp.concatenate([conv_weight.transpose(1, 0, 2), out_weight[None]], axis=0)
    gap = rows // 2
    dma = pltpu.SemaphoreType.DMA
    blk = (share, hidden)
    cz = chans // planes
    vmem = pltpu.VMEM
    both = lambda shape: [vmem(shape, BF16), vmem(shape, BF16)]
    outputs, input_grad, grads = pl.pallas_call(
        functools.partial(block_kernel, planes, factor),
        out_shape=(
            jax.ShapeDtypeStruct((rows, chans), BF16),
            jax.ShapeDtypeStruct((rows, chans), BF16),
            jax.ShapeDtypeStruct((4,) + blk, F32),
        ),
        in_specs=[pl.BlockSpec(memory_space=pltpu.VMEM)] * 3,
        out_specs=[pl.BlockSpec(memory_space=pltpu.VMEM)] * 3,
        scratch_shapes=[
            vmem((4, planes, 2, 2, 2) + blk, BF16),
            vmem((2, gap, chans), BF16),
            vmem((rows + 2 * gap, chans), BF16),
            vmem((4, rows, hidden), F32),
            vmem((rows, hidden), BF16),
            vmem((rows + 2 * gap, hidden), BF16),
            vmem((2, rows, cz), F32),
            vmem((2, 4, 2, 2, 2) + blk, F32),
            vmem((2, 4, 2, 2) + blk, F32),
            vmem((2, 2, 2) + blk, F32),
            vmem((2, 2, 2) + blk, F32),
            vmem((4,) + blk, F32),
            *both((planes, 4, 2, 2) + blk),
            *both((planes, 2, 2) + blk),
            *both((planes, 2, 2) + blk),
            *both((planes, 2) + blk),
            *both((planes, 2) + blk),
            *both((planes - 1, 4) + blk),
            dma((2, planes - 1)),
            dma((2, planes)),
            dma((2, planes)),
            dma((2, planes)),
            dma((2, planes)),
            dma((2, planes, 5)),
            dma((2, 2)),
            dma((2, 2)),
            dma((2, planes)),
            dma((2, planes)),
            dma((2, planes)),
            dma((2, planes)),
            dma((2, planes)),
            dma((2, planes - 1)),
            dma,
        ],
        compiler_params=pltpu.CompilerParams(
            collective_id=0, has_side_effects=True, vmem_limit_bytes=48 * 1024 * 1024
        ),
        cost_estimate=pl.CostEstimate(
            flops=2 * 12 * rows * chans * hidden, bytes_accessed=8 * rows * chans, transcendentals=0
        ),
    )(inputs[0], cotangent[0], w)
    return outputs[None], input_grad[None], grads[:3].transpose(1, 0, 2), grads[3]


def with_halo(cells, sides, width):
    for axis, dim in sides:
        count = lax.axis_size(axis)
        ends = count - 1
        head = lax.slice_in_dim(cells, 0, width, axis=dim)
        tail = lax.slice_in_dim(cells, cells.shape[dim] - width, cells.shape[dim], axis=dim)
        cells = jnp.concatenate(
            [
                lax.ppermute(tail, axis, [(i, (i + 1) % count) for i in range(ends)]),
                cells,
                lax.ppermute(head, axis, [((i + 1) % count, i) for i in range(ends)]),
            ],
            axis=dim,
        )
    return cells


def by_collectives(inputs, conv_weight, out_weight, cotangent):
    input_rows = inputs.shape[1]
    chans = inputs.shape[2]
    dilation_gap = input_rows // 2
    source = inputs[0]
    upstream = cotangent[0]
    wconv, wout = (
        lax.all_gather(conv_weight, ("dp", "seq"), axis=0, tiled=True),
        lax.all_gather(out_weight, ("dp", "seq"), axis=0, tiled=True),
    )
    hidden = wout.shape[1]
    wflat = wconv.reshape(chans, 3 * hidden)
    activated_value = jax.nn.gelu(source.astype(F32)).astype(BF16)
    widened_input = with_halo(activated_value, (("seq", 0),), dilation_gap)
    pre = jnp.zeros((input_rows, hidden), F32)
    for k in range(3):
        piece = jnp.dot(
            widened_input[k * dilation_gap : k * dilation_gap + input_rows],
            wconv[:, k, :],
            preferred_element_type=F32,
        )
        pre = pre + piece.astype(BF16).astype(F32)
    mid = jax.nn.gelu(pre).astype(BF16)
    outputs = (source.astype(F32) + jnp.dot(mid, wout.T, preferred_element_type=F32)).astype(BF16)
    dmid = jnp.dot(upstream, wout, preferred_element_type=F32)
    dpre = jax.vjp(jax.nn.gelu, pre)[1](dmid)[0].astype(BF16)
    wide = with_halo(dpre, (("seq", 0),), dilation_gap)
    shifted = jnp.concatenate(
        [wide[k * dilation_gap : k * dilation_gap + input_rows] for k in (2, 1, 0)], axis=1
    )
    dact = jnp.dot(shifted, wflat.T, preferred_element_type=F32)
    factor = 1.0 / math.sqrt(input_rows * lax.axis_size("seq") * lax.axis_size("dp"))
    conv_part = (
        jnp.einsum("pc,pk->ck", activated_value, shifted, preferred_element_type=F32) * factor
    ).reshape(chans, 3, hidden)
    out_part = jnp.einsum("pc,ph->ch", upstream, mid, preferred_element_type=F32) * factor
    input_grad = (
        upstream.astype(F32) + jax.vjp(jax.nn.gelu, source.astype(F32))[1](dact)[0]
    ).astype(BF16)
    conv_grad, out_grad = (
        lax.psum_scatter(conv_part, ("dp", "seq"), scatter_dimension=0, tiled=True),
        lax.psum_scatter(out_part, ("dp", "seq"), scatter_dimension=0, tiled=True),
    )
    return (outputs[None], input_grad[None], conv_grad, out_grad)


def solution(mesh):
    planes = mesh.shape["dp"] // 2

    def shards(inputs, conv_weight, out_weight, cotangent):
        aligned = conv_weight.shape[0] % 16 == 0 and mesh.shape["seq"] == 4 and 1 < planes <= 4
        if aligned:
            return fused(planes, inputs, conv_weight, out_weight, cotangent)
        return by_collectives(inputs, conv_weight, out_weight, cotangent)

    return jax.shard_map(
        shards,
        mesh=mesh,
        in_specs=(
            P("dp", "seq", None),
            P(("dp", "seq"), None, None),
            P(("dp", "seq"), None),
            P("dp", "seq", None),
        ),
        out_specs=(
            P("dp", "seq", None),
            P("dp", "seq", None),
            P(("dp", "seq"), None, None),
            P(("dp", "seq"), None),
        ),
        check_vma=False,
    )
```

```python
import functools
import math

import jax
import jax.numpy as jnp
from jax import lax
from jax.experimental import pallas as pl
from jax.experimental.pallas import tpu as pltpu
from jax.sharding import PartitionSpec as P

F32 = jnp.float32
BF16 = jnp.bfloat16
ALPHA = math.sqrt(2.0 / math.pi)
BETA = 0.044715


def gelu_and_slope(x):
    x2 = x * x
    t = jnp.tanh(ALPHA * x * (1.0 + BETA * x2))
    half = 0.5 * (1.0 + t)
    slope = half + 0.5 * x * (1.0 - t * t) * (ALPHA * (1.0 + 3.0 * BETA * x2))
    return x * half, slope


def gelu_only(x):
    t = jnp.tanh(ALPHA * x * (1.0 + BETA * (x * x)))
    return x * (0.5 * (1.0 + t))


def block_kernel(
    planes, factor,
    in_hbm, cot_hbm, w_ref,
    out_ref, ig_ref, cg_ref,
    in_ref, cot_ref, gat, xh, act, acc, mid, dpre, dacc, part, s0, s1a, s1b, s2,
    sb0, rb0, sb1a, rb1a, sb1b, rb1b, sb2a, rb2a, sb2b, rb2b, sb3, rb3,
    gz, gax, gay, gbx, gby, gc, hx, hd, q0, q1a, q1b, q2a, q2b, q3, qz, qloc,
):
    dp = lax.axis_index("dp")
    seq = lax.axis_index("seq")
    z, y = dp // 2, dp % 2
    x, c = seq // 2, seq % 2
    oy, ox, oc = 1 - y, 1 - x, 1 - c
    rows, chans = in_ref.shape
    gap = rows // 2
    cz = chans // planes
    hidden = w_ref.shape[2]
    seqs = 4
    ypeer = (z * 2 + oy, seq)
    xpeer = (dp, ox * 2 + c)
    cpeer = (dp, x * 2 + oc)
    diag = (dp, ox * 2 + oc)

    inner = ((z + 1) // 2) % 2
    flips = (z, z + 1 - 2 * (z % 2), lax.rem(z + 2, planes), planes - 1 - z)

    def zpeer(e):
        return (flips[e] * 2 + y, seq)

    def copy(src, dst, sems, peer):
        return pltpu.make_async_remote_copy(
            src_ref=src, dst_ref=dst, send_sem=sems[0], recv_sem=sems[1],
            device_id=peer, device_id_type=pl.DeviceIdType.MESH,
        )

    def pair(sem, *index):
        return sem.at[(0,) + index], sem.at[(1,) + index]

    def columns(i):
        return pl.ds(pl.multiple_of(i * cz, cz), cz)

    barrier = pltpu.get_barrier_semaphore()
    peers = [ypeer, xpeer, cpeer, diag] + [zpeer(d) for d in range(1, planes)]
    own = gat.at[:, z, y, x, c]
    mine = pltpu.make_async_copy(w_ref, own, qloc.at[0])
    load_in = pltpu.make_async_copy(in_hbm, in_ref, qloc.at[1])
    load_cot = pltpu.make_async_copy(cot_hbm, cot_ref, qloc.at[2])
    mine.start()
    load_in.start()
    load_cot.start()
    for peer in peers:
        pl.semaphore_signal(barrier, inc=1, device_id=peer, device_id_type=pl.DeviceIdType.MESH)
    mine.wait()
    pl.semaphore_wait(barrier, len(peers))

    sends = []

    def go(*copies):
        for one in copies:
            one.start()
            sends.append(one)
        return copies

    def arrived(copies):
        for one in copies:
            one.wait_recv()

    def at(n):
        if n < 2:
            return flips[n]
        near, far = (flips[3], flips[2]) if n == 2 else (flips[2], flips[3])
        return inner * near + (1 - inner) * far

    def plane(n, e, slot, order):
        piece = gat.at[:, at(n), y, x, c]
        return pltpu.make_async_remote_copy(
            src_ref=piece, dst_ref=piece, send_sem=qz.at[slot], recv_sem=gz.at[order - 1],
            device_id=zpeer(e), device_id_type=pl.DeviceIdType.MESH,
        )

    next_door = plane(0, 1, 0, 1)
    across = [plane(0, 3, 1, 2), plane(1, 3, 2, 3), plane(2, 1, 3, 2), plane(3, 1, 4, 3)]

    def landed(n):
        piece = gat.at[:, at(n), y, x, c]
        pltpu.make_async_remote_copy(
            src_ref=piece, dst_ref=piece, send_sem=qz.at[0], recv_sem=gz.at[n - 1],
            device_id=zpeer(1), device_id_type=pl.DeviceIdType.MESH,
        ).wait_recv()

    def inside(body):
        pl.when(inner == 1)(body)

    def outside(body):
        pl.when(inner == 0)(body)

    def spread(d):
        i = at(d)
        a = gat.at[0:2, i, y, x, c]
        b = gat.at[2:4, i, y, x, c]
        links = go(copy(a, a, pair(gay, d), ypeer), copy(b, b, pair(gax, d), xpeer))
        whole = gat.at[:, i, y, x, c]
        return links, go(copy(whole, whole, pair(gc, d, 0), cpeer))

    def spread_again(d):
        i = at(d)
        a = gat.at[0:2, i, :, x, c]
        b = gat.at[2:4, i, y, :, c]
        links = go(copy(a, a, pair(gbx, d), xpeer), copy(b, b, pair(gby, d), ypeer))
        a = gat.at[0:2, i, oy, x, c]
        b = gat.at[2:4, i, y, ox, c]
        return links, go(copy(a, a, pair(gc, d, 1), cpeer), copy(b, b, pair(gc, d, 2), cpeer))

    def share(d):
        i = at(d)
        a = gat.at[0:2, i, :, ox, c]
        b = gat.at[2:4, i, oy, :, c]
        return go(copy(a, a, pair(gc, d, 3), cpeer), copy(b, b, pair(gc, d, 4), cpeer))

    def neighbours(lower, upper, left, right, sem):
        to_right = copy(upper, left, pair(sem, 0), (dp, lax.rem(seq + 1, seqs)))
        to_left = copy(lower, right, pair(sem, 1), (dp, lax.rem(seq + seqs - 1, seqs)))
        return to_right, to_left

    def start_halo(halo):
        pl.when(seq < seqs - 1)(halo[0].start)
        pl.when(seq > 0)(halo[1].start)

    def wait_halo(halo):
        pl.when(seq > 0)(halo[0].wait_recv)
        pl.when(seq < seqs - 1)(halo[1].wait_recv)

    def wait_halo_sends(halo):
        pl.when(seq < seqs - 1)(halo[0].wait_send)
        pl.when(seq > 0)(halo[1].wait_send)

    tile = 32

    def activate_own():
        @pl.loop(0, rows // tile)
        def _(r):
            at_row = pl.multiple_of(r * tile, tile)
            value = in_ref[pl.ds(at_row, tile), :].astype(F32)
            act[pl.ds(pl.multiple_of(gap + at_row, tile), tile), :] = gelu_only(value).astype(BF16)

    def activate_halo():
        for side, start in ((0, 0), (1, gap + rows)):
            present = (seq > 0) if side == 0 else (seq < seqs - 1)

            @pl.when(present)
            def _():
                @pl.loop(0, gap // tile)
                def _(r):
                    at_row = pl.multiple_of(r * tile, tile)
                    value = xh[side, pl.ds(at_row, tile), :].astype(F32)
                    act[pl.ds(pl.multiple_of(start + at_row, tile), tile), :] = gelu_only(value).astype(BF16)

            @pl.when(jnp.logical_not(present))
            def _():
                act[start:start + gap, :] = jnp.zeros((gap, chans), BF16)
                dpre[start:start + gap, :] = jnp.zeros((gap, hidden), BF16)

    def weight(k, i):
        return gat[k, i].reshape(cz, hidden)

    def multiply(d):
        i = at(d)
        for k in range(4):
            left = act[k * gap:k * gap + rows, columns(i)] if k < 3 else cot_ref[:, columns(i)]
            value = jnp.dot(left, weight(k, i), preferred_element_type=F32)
            if d == 0:
                acc[k] = value
            else:
                acc[k] += value

    first, second, cores = {}, {}, {}
    halo = neighbours(in_ref.at[0:gap], in_ref.at[gap:rows], xh.at[0], xh.at[1], hx)

    def begin(n):
        first[n], cores[n] = spread(n)

    def carry_on(n):
        arrived(first[n])
        second[n], more = spread_again(n)
        cores[n] += more

    def hand_over(n):
        arrived(second[n])
        cores[n] += share(n)

    def use(n):
        arrived(cores[n])
        multiply(n)

    next_door.start()
    inside(across[0].start)
    begin(0)
    load_in.wait()
    start_halo(halo)
    activate_own()
    carry_on(0)
    landed(1)
    inside(across[1].start)
    begin(1)

    @inside
    def _():
        landed(2)
        across[2].start()

    carry_on(1)
    outside(lambda: landed(2))
    begin(2)

    @inside
    def _():
        landed(3)
        across[3].start()

    hand_over(0)
    carry_on(2)
    wait_halo(halo)
    activate_halo()
    load_cot.wait()
    use(0)
    outside(lambda: landed(3))
    begin(3)
    hand_over(1)
    use(1)
    carry_on(3)
    hand_over(2)
    use(2)
    hand_over(3)
    use(3)

    @pl.loop(0, rows // tile)
    def _(r):
        here = pl.ds(pl.multiple_of(r * tile, tile), tile)
        pre = acc[0, here, :].astype(BF16).astype(F32)
        pre += acc[1, here, :].astype(BF16).astype(F32)
        pre += acc[2, here, :].astype(BF16).astype(F32)
        value, slope = gelu_and_slope(pre)
        mid[here, :] = value.astype(BF16)
        dpre[pl.ds(pl.multiple_of(gap + r * tile, tile), tile), :] = (acc[3, here, :] * slope).astype(BF16)

    halo_d = neighbours(
        dpre.at[gap:2 * gap], dpre.at[2 * gap:3 * gap],
        dpre.at[0:gap], dpre.at[gap + rows:2 * gap + rows], hd,
    )
    start_halo(halo_d)

    def to(e):
        return flips[e]

    def partial(n, d):
        for k in range(4):
            if k < 3:
                left, right = act[k * gap:k * gap + rows, columns(to(d))], dpre[gap:gap + rows, :]
            else:
                left, right = cot_ref[:, columns(to(d))], mid[...]
            value = lax.dot_general(left, right, (((0,), (0,)), ((), ())), preferred_element_type=F32)
            part[n, k] = value.reshape(part.shape[2:])
        sb0[n] = part[n, :, :, :, oc].astype(BF16)
        return go(copy(sb0.at[n], rb0.at[n], pair(q0, n), cpeer))

    def sum_cores(n, copies):
        arrived(copies)
        s0[n] = part[n, :, :, :, c] + rb0[n].astype(F32)
        sb1a[n] = s0[n, 0:2, :, ox].astype(BF16)
        sb1b[n] = s0[n, 2:4, oy].astype(BF16)
        return go(
            copy(sb1a.at[n], rb1a.at[n], pair(q1a, n), xpeer),
            copy(sb1b.at[n], rb1b.at[n], pair(q1b, n), ypeer),
        )

    def sum_first(n, copies):
        arrived(copies)
        s1a[n] = s0[n, 0:2, :, x] + rb1a[n].astype(F32)
        s1b[n] = s0[n, 2:4, y] + rb1b[n].astype(F32)
        sb2a[n] = s1a[n, :, oy].astype(BF16)
        sb2b[n] = s1b[n, :, ox].astype(BF16)
        return go(
            copy(sb2a.at[n], rb2a.at[n], pair(q2a, n), ypeer),
            copy(sb2b.at[n], rb2b.at[n], pair(q2b, n), xpeer),
        )

    def sum_second(n, d, copies):
        arrived(copies)
        s2[0:2] = s1a[n, :, y] + rb2a[n].astype(F32)
        s2[2:4] = s1b[n, :, x] + rb2b[n].astype(F32)
        if d == 0:
            return ()
        sb3[n] = s2[...].astype(BF16)
        return go(copy(sb3.at[n], rb3.at[n], pair(q3, n), zpeer(d)))

    def finish_columns(j):
        here = slice(j * cz, (j + 1) * cz)
        nt = (((1,), (1,)), ((), ()))
        total = lax.dot_general(dpre[2 * gap:4 * gap, :], weight(0, j), nt, preferred_element_type=F32)
        total += lax.dot_general(dpre[gap:3 * gap, :], weight(1, j), nt, preferred_element_type=F32)
        total += lax.dot_general(dpre[0:2 * gap, :], weight(2, j), nt, preferred_element_type=F32)
        dacc[0] = total
        dacc[1] = lax.dot_general(mid[...], weight(3, j), nt, preferred_element_type=F32)

        @pl.loop(0, rows // tile)
        def _(r):
            at_row = pl.ds(pl.multiple_of(r * tile, tile), tile)
            source = in_ref[at_row, here].astype(F32)
            out_ref[at_row, here] = (source + dacc[1, at_row, :]).astype(BF16)
            slope = gelu_and_slope(source)[1]
            ig_ref[at_row, here] = (cot_ref[at_row, here].astype(F32) + dacc[0, at_row, :] * slope).astype(BF16)

    order = [2, 3, 1, 0]
    r0, r1, r2, r3 = {}, {}, {}, []
    fills = list(range(planes))
    for t in range(planes + 4):
        if t < planes:
            r0[t] = partial(t, order[t])
        if 0 <= t - 1 < planes:
            r1[t - 1] = sum_cores(t - 1, r0[t - 1])
        if 0 <= t - 3 < planes:
            r2[t - 3] = sum_first(t - 3, r1[t - 3])
        if 0 <= t - 4 < planes:
            r3 += sum_second(t - 4, order[t - 4], r2[t - 4])
        if t >= 2 and fills:
            if t == 2:
                wait_halo(halo_d)
            finish_columns(fills.pop(0))
    for j in fills:
        finish_columns(j)
    arrived(r3)
    total = s2[...]
    for n in range(planes - 1):
        total += rb3[n].astype(F32)
    cg_ref[...] = total * factor

    for one in sends:
        one.wait_send()
    next_door.wait_send()

    @inside
    def _():
        for one in across:
            one.wait_send()

    wait_halo_sends(halo)
    wait_halo_sends(halo_d)


def fused(planes, inputs, conv_weight, out_weight, cotangent):
    rows, chans = inputs.shape[1:]
    share, taps, hidden = conv_weight.shape
    factor = 1.0 / math.sqrt(rows * lax.axis_size("seq") * lax.axis_size("dp"))
    w = jnp.concatenate([conv_weight.transpose(1, 0, 2), out_weight[None]], axis=0)
    gap = rows // 2
    dma = pltpu.SemaphoreType.DMA
    blk = (share, hidden)
    cz = chans // planes
    vmem = pltpu.VMEM
    both = lambda shape: [vmem(shape, BF16), vmem(shape, BF16)]
    outputs, input_grad, grads = pl.pallas_call(
        functools.partial(block_kernel, planes, factor),
        out_shape=(
            jax.ShapeDtypeStruct((rows, chans), BF16),
            jax.ShapeDtypeStruct((rows, chans), BF16),
            jax.ShapeDtypeStruct((4,) + blk, F32),
        ),
        in_specs=[pl.BlockSpec(memory_space=pl.ANY)] * 2 + [pl.BlockSpec(memory_space=pltpu.VMEM)],
        out_specs=[pl.BlockSpec(memory_space=pltpu.VMEM)] * 3,
        scratch_shapes=[
            vmem((rows, chans), BF16),
            vmem((rows, chans), BF16),
            vmem((4, planes, 2, 2, 2) + blk, BF16),
            vmem((2, gap, chans), BF16),
            vmem((rows + 2 * gap, chans), BF16),
            vmem((4, rows, hidden), F32),
            vmem((rows, hidden), BF16),
            vmem((rows + 2 * gap, hidden), BF16),
            vmem((2, rows, cz), F32),
            vmem((planes, 4, 2, 2, 2) + blk, F32),
            vmem((planes, 4, 2, 2) + blk, F32),
            vmem((planes, 2, 2) + blk, F32),
            vmem((planes, 2, 2) + blk, F32),
            vmem((4,) + blk, F32),
            *both((planes, 4, 2, 2) + blk),
            *both((planes, 2, 2) + blk),
            *both((planes, 2, 2) + blk),
            *both((planes, 2) + blk),
            *both((planes, 2) + blk),
            *both((planes - 1, 4) + blk),
            dma((planes - 1,)),
            dma((2, planes)),
            dma((2, planes)),
            dma((2, planes)),
            dma((2, planes)),
            dma((2, planes, 5)),
            dma((2, 2)),
            dma((2, 2)),
            dma((2, planes)),
            dma((2, planes)),
            dma((2, planes)),
            dma((2, planes)),
            dma((2, planes)),
            dma((2, planes - 1)),
            dma((5,)),
            dma((3,)),
        ],
        compiler_params=pltpu.CompilerParams(
            collective_id=0, has_side_effects=True, vmem_limit_bytes=48 * 1024 * 1024
        ),
        cost_estimate=pl.CostEstimate(
            flops=2 * 12 * rows * chans * hidden, bytes_accessed=8 * rows * chans, transcendentals=0
        ),
    )(inputs[0], cotangent[0], w)
    return outputs[None], input_grad[None], grads[:3].transpose(1, 0, 2), grads[3]


def with_halo(cells, sides, width):
    for axis, dim in sides:
        count = lax.axis_size(axis)
        ends = count - 1
        head = lax.slice_in_dim(cells, 0, width, axis=dim)
        tail = lax.slice_in_dim(cells, cells.shape[dim] - width, cells.shape[dim], axis=dim)
        cells = jnp.concatenate(
            [
                lax.ppermute(tail, axis, [(i, (i + 1) % count) for i in range(ends)]),
                cells,
                lax.ppermute(head, axis, [((i + 1) % count, i) for i in range(ends)]),
            ],
            axis=dim,
        )
    return cells


def by_collectives(inputs, conv_weight, out_weight, cotangent):
    input_rows = inputs.shape[1]
    chans = inputs.shape[2]
    dilation_gap = input_rows // 2
    source = inputs[0]
    upstream = cotangent[0]
    wconv, wout = (
        lax.all_gather(conv_weight, ("dp", "seq"), axis=0, tiled=True),
        lax.all_gather(out_weight, ("dp", "seq"), axis=0, tiled=True),
    )
    hidden = wout.shape[1]
    wflat = wconv.reshape(chans, 3 * hidden)
    activated_value = jax.nn.gelu(source.astype(F32)).astype(BF16)
    widened_input = with_halo(activated_value, (("seq", 0),), dilation_gap)
    pre = jnp.zeros((input_rows, hidden), F32)
    for k in range(3):
        piece = jnp.dot(
            widened_input[k * dilation_gap : k * dilation_gap + input_rows],
            wconv[:, k, :],
            preferred_element_type=F32,
        )
        pre = pre + piece.astype(BF16).astype(F32)
    mid = jax.nn.gelu(pre).astype(BF16)
    outputs = (source.astype(F32) + jnp.dot(mid, wout.T, preferred_element_type=F32)).astype(BF16)
    dmid = jnp.dot(upstream, wout, preferred_element_type=F32)
    dpre = jax.vjp(jax.nn.gelu, pre)[1](dmid)[0].astype(BF16)
    wide = with_halo(dpre, (("seq", 0),), dilation_gap)
    shifted = jnp.concatenate(
        [wide[k * dilation_gap : k * dilation_gap + input_rows] for k in (2, 1, 0)], axis=1
    )
    dact = jnp.dot(shifted, wflat.T, preferred_element_type=F32)
    factor = 1.0 / math.sqrt(input_rows * lax.axis_size("seq") * lax.axis_size("dp"))
    conv_part = (
        jnp.einsum("pc,pk->ck", activated_value, shifted, preferred_element_type=F32) * factor
    ).reshape(chans, 3, hidden)
    out_part = jnp.einsum("pc,ph->ch", upstream, mid, preferred_element_type=F32) * factor
    input_grad = (
        upstream.astype(F32) + jax.vjp(jax.nn.gelu, source.astype(F32))[1](dact)[0]
    ).astype(BF16)
    conv_grad, out_grad = (
        lax.psum_scatter(conv_part, ("dp", "seq"), scatter_dimension=0, tiled=True),
        lax.psum_scatter(out_part, ("dp", "seq"), scatter_dimension=0, tiled=True),
    )
    return (outputs[None], input_grad[None], conv_grad, out_grad)


def solution(mesh):
    planes = mesh.shape["dp"] // 2

    def shards(inputs, conv_weight, out_weight, cotangent):
        aligned = conv_weight.shape[0] % 16 == 0 and mesh.shape["seq"] == 4 and planes == 4
        if aligned:
            return fused(planes, inputs, conv_weight, out_weight, cotangent)
        return by_collectives(inputs, conv_weight, out_weight, cotangent)

    return jax.shard_map(
        shards,
        mesh=mesh,
        in_specs=(
            P("dp", "seq", None),
            P(("dp", "seq"), None, None),
            P(("dp", "seq"), None),
            P("dp", "seq", None),
        ),
        out_specs=(
            P("dp", "seq", None),
            P("dp", "seq", None),
            P(("dp", "seq"), None, None),
            P(("dp", "seq"), None),
        ),
        check_vma=False,
    )
```

```python
import functools
import math

import jax
import jax.numpy as jnp
from jax import lax
from jax.experimental import pallas as pl
from jax.experimental.pallas import tpu as pltpu
from jax.sharding import PartitionSpec as P

F32 = jnp.float32
BF16 = jnp.bfloat16
ALPHA = math.sqrt(2.0 / math.pi)
BETA = 0.044715


def gelu_and_slope(x):
    x2 = x * x
    t = jnp.tanh(ALPHA * x * (1.0 + BETA * x2))
    half = 0.5 * (1.0 + t)
    slope = half + 0.5 * x * (1.0 - t * t) * (ALPHA * (1.0 + 3.0 * BETA * x2))
    return x * half, slope


def gelu_only(x):
    t = jnp.tanh(ALPHA * x * (1.0 + BETA * (x * x)))
    return x * (0.5 * (1.0 + t))


def block_kernel(
    planes, factor,
    in_hbm, cot_hbm, w_ref,
    out_hbm, ig_hbm, cg_ref,
    in_ref, cot_ref, out_ref, ig_ref, gat, xh, act, acc, mid, dpre, dacc, part, s0, s1a, s1b, s2,
    sb0, rb0, sb1a, rb1a, sb1b, rb1b, sb2a, rb2a, sb2b, rb2b, sb3, rb3,
    gz, gax, gay, gbx, gby, gc, hx, hd, q0, q1a, q1b, q2a, q2b, q3, qz, qloc, qout,
):
    dp = lax.axis_index("dp")
    seq = lax.axis_index("seq")
    z, y = dp // 2, dp % 2
    x, c = seq // 2, seq % 2
    oy, ox, oc = 1 - y, 1 - x, 1 - c
    rows, chans = in_ref.shape
    gap = rows // 2
    cz = chans // planes
    hidden = w_ref.shape[2]
    seqs = 4
    ypeer = (z * 2 + oy, seq)
    xpeer = (dp, ox * 2 + c)
    cpeer = (dp, x * 2 + oc)
    diag = (dp, ox * 2 + oc)

    flips = (z, z + 1 - 2 * (z % 2), lax.rem(z + 2, planes), planes - 1 - z)

    def zpeer(e):
        return (flips[e] * 2 + y, seq)

    def copy(src, dst, sems, peer):
        return pltpu.make_async_remote_copy(
            src_ref=src, dst_ref=dst, send_sem=sems[0], recv_sem=sems[1],
            device_id=peer, device_id_type=pl.DeviceIdType.MESH,
        )

    def pair(sem, *index):
        return sem.at[(0,) + index], sem.at[(1,) + index]

    def columns(i):
        return pl.ds(pl.multiple_of(i * cz, cz), cz)

    barrier = pltpu.get_barrier_semaphore()
    peers = [ypeer, xpeer, cpeer, diag] + [zpeer(d) for d in range(1, planes)]
    own = gat.at[:, z, y, x, c]
    mine = pltpu.make_async_copy(w_ref, own, qloc.at[0])
    load_in = pltpu.make_async_copy(in_hbm, in_ref, qloc.at[1])
    load_cot = pltpu.make_async_copy(cot_hbm, cot_ref, qloc.at[2])
    mine.start()
    load_in.start()
    load_cot.start()
    for peer in peers:
        pl.semaphore_signal(barrier, inc=1, device_id=peer, device_id_type=pl.DeviceIdType.MESH)
    mine.wait()
    pl.semaphore_wait(barrier, len(peers))

    sends = []

    def go(*copies):
        for one in copies:
            one.start()
            sends.append(one)
        return copies

    def arrived(copies):
        for one in copies:
            one.wait_recv()

    def at(n):
        return flips[n]

    def taps(n):
        return 4 if n == 0 else 3

    def spread(n):
        i = at(n)
        a = gat.at[0:2, i, y, x, c]
        b = gat.at[2:taps(n), i, y, x, c]
        links = go(copy(a, a, pair(gay, n), ypeer), copy(b, b, pair(gax, n), xpeer))
        whole = gat.at[0:taps(n), i, y, x, c]
        return links, go(copy(whole, whole, pair(gc, n, 0), cpeer))

    def spread_again(n):
        i = at(n)
        a = gat.at[0:2, i, :, x, c]
        b = gat.at[2:taps(n), i, y, :, c]
        links = go(copy(a, a, pair(gbx, n), xpeer), copy(b, b, pair(gby, n), ypeer))
        a = gat.at[0:2, i, oy, x, c]
        b = gat.at[2:taps(n), i, y, ox, c]
        return links, go(copy(a, a, pair(gc, n, 1), cpeer), copy(b, b, pair(gc, n, 2), cpeer))

    def share(n):
        i = at(n)
        a = gat.at[0:2, i, :, ox, c]
        b = gat.at[2:taps(n), i, oy, :, c]
        return go(copy(a, a, pair(gc, n, 3), cpeer), copy(b, b, pair(gc, n, 4), cpeer))

    own_taps = gat.at[0:3, z, y, x, c]
    zs = [()] + [
        go(copy(own_taps, own_taps, pair(gz, n - 1), zpeer(n))) for n in range(1, planes)
    ]

    def send_projection():
        a = gat.at[3, z, :, :, c]
        return [()] + [go(copy(a, a, pair(qz, n - 1), zpeer(n))) for n in range(1, planes)]

    def share_projection(n, copies):
        arrived(copies)
        a = gat.at[3, at(n), :, :, c]
        return go(copy(a, a, pair(gc, n, 5), cpeer))

    def neighbours(lower, upper, left, right, sem):
        to_right = copy(upper, left, pair(sem, 0), (dp, lax.rem(seq + 1, seqs)))
        to_left = copy(lower, right, pair(sem, 1), (dp, lax.rem(seq + seqs - 1, seqs)))
        return to_right, to_left

    def start_halo(halo):
        pl.when(seq < seqs - 1)(halo[0].start)
        pl.when(seq > 0)(halo[1].start)

    def wait_halo(halo):
        pl.when(seq > 0)(halo[0].wait_recv)
        pl.when(seq < seqs - 1)(halo[1].wait_recv)

    def wait_halo_sends(halo):
        pl.when(seq < seqs - 1)(halo[0].wait_send)
        pl.when(seq > 0)(halo[1].wait_send)

    tile = 32

    def activate_own():
        @pl.loop(0, rows // tile)
        def _(r):
            at_row = pl.multiple_of(r * tile, tile)
            value = in_ref[pl.ds(at_row, tile), :].astype(F32)
            act[pl.ds(pl.multiple_of(gap + at_row, tile), tile), :] = gelu_only(value).astype(BF16)

    def activate_halo():
        for side, start in ((0, 0), (1, gap + rows)):
            present = (seq > 0) if side == 0 else (seq < seqs - 1)

            @pl.when(present)
            def _():
                @pl.loop(0, gap // tile)
                def _(r):
                    at_row = pl.multiple_of(r * tile, tile)
                    value = xh[side, pl.ds(at_row, tile), :].astype(F32)
                    act[pl.ds(pl.multiple_of(start + at_row, tile), tile), :] = gelu_only(value).astype(BF16)

            @pl.when(jnp.logical_not(present))
            def _():
                act[start:start + gap, :] = jnp.zeros((gap, chans), BF16)
                dpre[start:start + gap, :] = jnp.zeros((gap, hidden), BF16)

    def weight(k, i):
        return gat[k, i].reshape(cz, hidden)

    def multiply(n, some):
        i = at(n)
        for k in some:
            left = act[k * gap:k * gap + rows, columns(i)] if k < 3 else cot_ref[:, columns(i)]
            value = jnp.dot(left, weight(k, i), preferred_element_type=F32)
            if n == 0:
                acc[k] = value
            else:
                acc[k] += value

    first, second, cores = {}, {}, {}
    halo = neighbours(in_ref.at[0:gap], in_ref.at[gap:rows], xh.at[0], xh.at[1], hx)

    def begin(n):
        first[n], cores[n] = spread(n)

    def carry_on(n):
        arrived(first[n])
        second[n], more = spread_again(n)
        cores[n] += more

    def hand_over(n):
        arrived(second[n])
        cores[n] += share(n)

    def use(n):
        arrived(cores[n])
        multiply(n, range(taps(n)))

    begin(0)
    load_in.wait()
    start_halo(halo)
    activate_own()
    carry_on(0)
    hand_over(0)
    projection = send_projection()
    for n in range(1, planes):
        arrived(zs[n])
        begin(n)
        if n > 1:
            carry_on(n - 1)
    wait_halo(halo)
    activate_halo()
    hand_over(1)
    carry_on(planes - 1)
    load_cot.wait()
    use(0)
    use(1)
    for n in range(2, planes):
        hand_over(n)
        use(n)
    rest = [share_projection(n, projection[n]) for n in range(1, planes)]
    for n in range(1, planes):
        arrived(rest[n - 1])
        multiply(n, (3,))

    @pl.loop(0, rows // tile)
    def _(r):
        here = pl.ds(pl.multiple_of(r * tile, tile), tile)
        pre = acc[0, here, :].astype(BF16).astype(F32)
        pre += acc[1, here, :].astype(BF16).astype(F32)
        pre += acc[2, here, :].astype(BF16).astype(F32)
        value, slope = gelu_and_slope(pre)
        mid[here, :] = value.astype(BF16)
        dpre[pl.ds(pl.multiple_of(gap + r * tile, tile), tile), :] = (acc[3, here, :] * slope).astype(BF16)

    halo_d = neighbours(
        dpre.at[gap:2 * gap], dpre.at[2 * gap:3 * gap],
        dpre.at[0:gap], dpre.at[gap + rows:2 * gap + rows], hd,
    )
    start_halo(halo_d)

    def to(e):
        return flips[e]

    def partial(n, d):
        for k in range(4):
            if k < 3:
                left, right = act[k * gap:k * gap + rows, columns(to(d))], dpre[gap:gap + rows, :]
            else:
                left, right = cot_ref[:, columns(to(d))], mid[...]
            value = lax.dot_general(left, right, (((0,), (0,)), ((), ())), preferred_element_type=F32)
            part[n, k] = value.reshape(part.shape[2:])
        sb0[n] = part[n, :, :, :, oc].astype(BF16)
        return go(copy(sb0.at[n], rb0.at[n], pair(q0, n), cpeer))

    def sum_cores(n, copies):
        arrived(copies)
        s0[n] = part[n, :, :, :, c] + rb0[n].astype(F32)
        sb1a[n] = s0[n, 0:2, :, ox].astype(BF16)
        sb1b[n] = s0[n, 2:4, oy].astype(BF16)
        return go(
            copy(sb1a.at[n], rb1a.at[n], pair(q1a, n), xpeer),
            copy(sb1b.at[n], rb1b.at[n], pair(q1b, n), ypeer),
        )

    def sum_first(n, copies):
        arrived(copies)
        s1a[n] = s0[n, 0:2, :, x] + rb1a[n].astype(F32)
        s1b[n] = s0[n, 2:4, y] + rb1b[n].astype(F32)
        sb2a[n] = s1a[n, :, oy].astype(BF16)
        sb2b[n] = s1b[n, :, ox].astype(BF16)
        return go(
            copy(sb2a.at[n], rb2a.at[n], pair(q2a, n), ypeer),
            copy(sb2b.at[n], rb2b.at[n], pair(q2b, n), xpeer),
        )

    def sum_second(n, d, copies):
        arrived(copies)
        s2[0:2] = s1a[n, :, y] + rb2a[n].astype(F32)
        s2[2:4] = s1b[n, :, x] + rb2b[n].astype(F32)
        if d == 0:
            return ()
        sb3[n] = s2[...].astype(BF16)
        return go(copy(sb3.at[n], rb3.at[n], pair(q3, n), zpeer(d)))

    def finish_columns(j):
        here = slice(j * cz, (j + 1) * cz)
        nt = (((1,), (1,)), ((), ()))
        total = lax.dot_general(dpre[2 * gap:4 * gap, :], weight(0, j), nt, preferred_element_type=F32)
        total += lax.dot_general(dpre[gap:3 * gap, :], weight(1, j), nt, preferred_element_type=F32)
        total += lax.dot_general(dpre[0:2 * gap, :], weight(2, j), nt, preferred_element_type=F32)
        dacc[0] = total
        dacc[1] = lax.dot_general(mid[...], weight(3, j), nt, preferred_element_type=F32)

        @pl.loop(0, rows // tile)
        def _(r):
            at_row = pl.ds(pl.multiple_of(r * tile, tile), tile)
            source = in_ref[at_row, here].astype(F32)
            out_ref[at_row, here] = (source + dacc[1, at_row, :]).astype(BF16)
            slope = gelu_and_slope(source)[1]
            ig_ref[at_row, here] = (cot_ref[at_row, here].astype(F32) + dacc[0, at_row, :] * slope).astype(BF16)

    leaving = []

    def leave(j):
        here = pl.ds(j * cz, cz)
        for n, (ref, hbm) in enumerate(((out_ref, out_hbm), (ig_ref, ig_hbm))):
            one = pltpu.make_async_copy(ref.at[:, here], hbm.at[:, here], qout.at[n, j])
            one.start()
            leaving.append(one)

    order = [2, 3, 1, 0]
    r0, r1, r2, r3 = {}, {}, {}, []
    fills = list(range(planes))
    for t in range(planes + 4):
        if t < planes:
            r0[t] = partial(t, order[t])
        if 0 <= t - 1 < planes:
            r1[t - 1] = sum_cores(t - 1, r0[t - 1])
        if 0 <= t - 3 < planes:
            r2[t - 3] = sum_first(t - 3, r1[t - 3])
        if 0 <= t - 4 < planes:
            r3 += sum_second(t - 4, order[t - 4], r2[t - 4])
        if t >= 2 and fills:
            if t == 2:
                wait_halo(halo_d)
            finish_columns(fills[0])
            leave(fills.pop(0))
    for j in fills:
        finish_columns(j)
        leave(j)
    arrived(r3)
    total = s2[...]
    for n in range(planes - 1):
        total += rb3[n].astype(F32)
    cg_ref[...] = total * factor

    for one in sends:
        one.wait_send()
    for one in leaving:
        one.wait()
    wait_halo_sends(halo)
    wait_halo_sends(halo_d)


def fused(planes, inputs, conv_weight, out_weight, cotangent):
    rows, chans = inputs.shape[1:]
    share, taps, hidden = conv_weight.shape
    factor = 1.0 / math.sqrt(rows * lax.axis_size("seq") * lax.axis_size("dp"))
    w = jnp.concatenate([conv_weight.transpose(1, 0, 2), out_weight[None]], axis=0)
    gap = rows // 2
    dma = pltpu.SemaphoreType.DMA
    blk = (share, hidden)
    cz = chans // planes
    vmem = pltpu.VMEM
    both = lambda shape: [vmem(shape, BF16), vmem(shape, BF16)]
    outputs, input_grad, grads = pl.pallas_call(
        functools.partial(block_kernel, planes, factor),
        out_shape=(
            jax.ShapeDtypeStruct((rows, chans), BF16),
            jax.ShapeDtypeStruct((rows, chans), BF16),
            jax.ShapeDtypeStruct((4,) + blk, F32),
        ),
        in_specs=[pl.BlockSpec(memory_space=pl.ANY)] * 2 + [pl.BlockSpec(memory_space=pltpu.VMEM)],
        out_specs=[pl.BlockSpec(memory_space=pl.ANY)] * 2 + [pl.BlockSpec(memory_space=pltpu.VMEM)],
        scratch_shapes=[
            vmem((rows, chans), BF16),
            vmem((rows, chans), BF16),
            vmem((rows, chans), BF16),
            vmem((rows, chans), BF16),
            vmem((4, planes, 2, 2, 2) + blk, BF16),
            vmem((2, gap, chans), BF16),
            vmem((rows + 2 * gap, chans), BF16),
            vmem((4, rows, hidden), F32),
            vmem((rows, hidden), BF16),
            vmem((rows + 2 * gap, hidden), BF16),
            vmem((2, rows, cz), F32),
            vmem((planes, 4, 2, 2, 2) + blk, F32),
            vmem((planes, 4, 2, 2) + blk, F32),
            vmem((planes, 2, 2) + blk, F32),
            vmem((planes, 2, 2) + blk, F32),
            vmem((4,) + blk, F32),
            *both((planes, 4, 2, 2) + blk),
            *both((planes, 2, 2) + blk),
            *both((planes, 2, 2) + blk),
            *both((planes, 2) + blk),
            *both((planes, 2) + blk),
            *both((planes - 1, 4) + blk),
            dma((2, planes - 1)),
            dma((2, planes)),
            dma((2, planes)),
            dma((2, planes)),
            dma((2, planes)),
            dma((2, planes, 6)),
            dma((2, 2)),
            dma((2, 2)),
            dma((2, planes)),
            dma((2, planes)),
            dma((2, planes)),
            dma((2, planes)),
            dma((2, planes)),
            dma((2, planes - 1)),
            dma((2, planes - 1)),
            dma((3,)),
            dma((2, planes)),
        ],
        compiler_params=pltpu.CompilerParams(
            collective_id=0, has_side_effects=True, vmem_limit_bytes=48 * 1024 * 1024
        ),
        cost_estimate=pl.CostEstimate(
            flops=2 * 12 * rows * chans * hidden, bytes_accessed=8 * rows * chans, transcendentals=0
        ),
    )(inputs[0], cotangent[0], w)
    return outputs[None], input_grad[None], grads[:3].transpose(1, 0, 2), grads[3]


def with_halo(cells, sides, width):
    for axis, dim in sides:
        count = lax.axis_size(axis)
        ends = count - 1
        head = lax.slice_in_dim(cells, 0, width, axis=dim)
        tail = lax.slice_in_dim(cells, cells.shape[dim] - width, cells.shape[dim], axis=dim)
        cells = jnp.concatenate(
            [
                lax.ppermute(tail, axis, [(i, (i + 1) % count) for i in range(ends)]),
                cells,
                lax.ppermute(head, axis, [((i + 1) % count, i) for i in range(ends)]),
            ],
            axis=dim,
        )
    return cells


def by_collectives(inputs, conv_weight, out_weight, cotangent):
    input_rows = inputs.shape[1]
    chans = inputs.shape[2]
    dilation_gap = input_rows // 2
    source = inputs[0]
    upstream = cotangent[0]
    wconv, wout = (
        lax.all_gather(conv_weight, ("dp", "seq"), axis=0, tiled=True),
        lax.all_gather(out_weight, ("dp", "seq"), axis=0, tiled=True),
    )
    hidden = wout.shape[1]
    wflat = wconv.reshape(chans, 3 * hidden)
    activated_value = jax.nn.gelu(source.astype(F32)).astype(BF16)
    widened_input = with_halo(activated_value, (("seq", 0),), dilation_gap)
    pre = jnp.zeros((input_rows, hidden), F32)
    for k in range(3):
        piece = jnp.dot(
            widened_input[k * dilation_gap : k * dilation_gap + input_rows],
            wconv[:, k, :],
            preferred_element_type=F32,
        )
        pre = pre + piece.astype(BF16).astype(F32)
    mid = jax.nn.gelu(pre).astype(BF16)
    outputs = (source.astype(F32) + jnp.dot(mid, wout.T, preferred_element_type=F32)).astype(BF16)
    dmid = jnp.dot(upstream, wout, preferred_element_type=F32)
    dpre = jax.vjp(jax.nn.gelu, pre)[1](dmid)[0].astype(BF16)
    wide = with_halo(dpre, (("seq", 0),), dilation_gap)
    shifted = jnp.concatenate(
        [wide[k * dilation_gap : k * dilation_gap + input_rows] for k in (2, 1, 0)], axis=1
    )
    dact = jnp.dot(shifted, wflat.T, preferred_element_type=F32)
    factor = 1.0 / math.sqrt(input_rows * lax.axis_size("seq") * lax.axis_size("dp"))
    conv_part = (
        jnp.einsum("pc,pk->ck", activated_value, shifted, preferred_element_type=F32) * factor
    ).reshape(chans, 3, hidden)
    out_part = jnp.einsum("pc,ph->ch", upstream, mid, preferred_element_type=F32) * factor
    input_grad = (
        upstream.astype(F32) + jax.vjp(jax.nn.gelu, source.astype(F32))[1](dact)[0]
    ).astype(BF16)
    conv_grad, out_grad = (
        lax.psum_scatter(conv_part, ("dp", "seq"), scatter_dimension=0, tiled=True),
        lax.psum_scatter(out_part, ("dp", "seq"), scatter_dimension=0, tiled=True),
    )
    return (outputs[None], input_grad[None], conv_grad, out_grad)


def solution(mesh):
    planes = mesh.shape["dp"] // 2

    def shards(inputs, conv_weight, out_weight, cotangent):
        aligned = conv_weight.shape[0] % 16 == 0 and mesh.shape["seq"] == 4 and planes == 4
        if aligned:
            return fused(planes, inputs, conv_weight, out_weight, cotangent)
        return by_collectives(inputs, conv_weight, out_weight, cotangent)

    return jax.shard_map(
        shards,
        mesh=mesh,
        in_specs=(
            P("dp", "seq", None),
            P(("dp", "seq"), None, None),
            P(("dp", "seq"), None),
            P("dp", "seq", None),
        ),
        out_specs=(
            P("dp", "seq", None),
            P("dp", "seq", None),
            P(("dp", "seq"), None, None),
            P(("dp", "seq"), None),
        ),
        check_vma=False,
    )
```

```python
import functools
import math

import jax
import jax.numpy as jnp
from jax import lax
from jax.experimental import pallas as pl
from jax.experimental.pallas import tpu as pltpu
from jax.sharding import PartitionSpec as P

F32 = jnp.float32
BF16 = jnp.bfloat16
ALPHA = math.sqrt(2.0 / math.pi)
BETA = 0.044715


def gelu_and_slope(x):
    x2 = x * x
    t = jnp.tanh(ALPHA * x * (1.0 + BETA * x2))
    half = 0.5 * (1.0 + t)
    slope = half + 0.5 * x * (1.0 - t * t) * (ALPHA * (1.0 + 3.0 * BETA * x2))
    return x * half, slope


def gelu_only(x):
    t = jnp.tanh(ALPHA * x * (1.0 + BETA * (x * x)))
    return x * (0.5 * (1.0 + t))


def block_kernel(
    planes, factor,
    in_hbm, cot_hbm, w_ref,
    out_ref, ig_ref, cg_ref,
    in_ref, cot_ref, gat, xh, act, acc, mid, dpre, dacc, part, s0, s1a, s1b, s2,
    sb0, rb0, sb1a, rb1a, sb1b, rb1b, sb2a, rb2a, sb2b, rb2b, sb3, rb3,
    gz, gax, gay, gbx, gby, gc, hx, hd, q0, q1a, q1b, q2a, q2b, q3, qloc,
):
    dp = lax.axis_index("dp")
    seq = lax.axis_index("seq")
    z, y = dp // 2, dp % 2
    x, c = seq // 2, seq % 2
    oy, ox, oc = 1 - y, 1 - x, 1 - c
    rows, chans = in_ref.shape
    gap = rows // 2
    cz = chans // planes
    hidden = w_ref.shape[2]
    seqs = 4
    ypeer = (z * 2 + oy, seq)
    xpeer = (dp, ox * 2 + c)
    cpeer = (dp, x * 2 + oc)
    diag = (dp, ox * 2 + oc)

    def zpeer(d):
        return (lax.rem(z + d, planes) * 2 + y, seq)

    def copy(src, dst, sems, peer):
        return pltpu.make_async_remote_copy(
            src_ref=src, dst_ref=dst, send_sem=sems[0], recv_sem=sems[1],
            device_id=peer, device_id_type=pl.DeviceIdType.MESH,
        )

    def pair(sem, *index):
        return sem.at[(0,) + index], sem.at[(1,) + index]

    def columns(i):
        return pl.ds(pl.multiple_of(i * cz, cz), cz)

    barrier = pltpu.get_barrier_semaphore()
    peers = [ypeer, xpeer, cpeer, diag] + [zpeer(d) for d in range(1, planes)]
    own = gat.at[:, z, y, x, c]
    mine = pltpu.make_async_copy(w_ref, own, qloc.at[0])
    load_in = pltpu.make_async_copy(in_hbm, in_ref, qloc.at[1])
    load_cot = pltpu.make_async_copy(cot_hbm, cot_ref, qloc.at[2])
    mine.start()
    load_in.start()
    load_cot.start()
    for peer in peers:
        pl.semaphore_signal(barrier, inc=1, device_id=peer, device_id_type=pl.DeviceIdType.MESH)
    mine.wait()
    pl.semaphore_wait(barrier, len(peers))

    sends = []

    def go(*copies):
        for one in copies:
            one.start()
            sends.append(one)
        return copies

    def arrived(copies):
        for one in copies:
            one.wait_recv()

    def at(d):
        return lax.rem(z + planes - d, planes)

    zs = [None] + [
        go(copy(own, own, pair(gz, d - 1), zpeer(d)))
        for d in range(1, planes)
    ]

    def spread(d):
        i = at(d)
        a = gat.at[0:2, i, y, x, c]
        b = gat.at[2:4, i, y, x, c]
        links = go(copy(a, a, pair(gay, d), ypeer), copy(b, b, pair(gax, d), xpeer))
        whole = gat.at[:, i, y, x, c]
        return links, go(copy(whole, whole, pair(gc, d, 0), cpeer))

    def spread_again(d):
        i = at(d)
        a = gat.at[0:2, i, :, x, c]
        b = gat.at[2:4, i, y, :, c]
        links = go(copy(a, a, pair(gbx, d), xpeer), copy(b, b, pair(gby, d), ypeer))
        a = gat.at[0:2, i, oy, x, c]
        b = gat.at[2:4, i, y, ox, c]
        return links, go(copy(a, a, pair(gc, d, 1), cpeer), copy(b, b, pair(gc, d, 2), cpeer))

    def share(d):
        i = at(d)
        a = gat.at[0:2, i, :, ox, c]
        b = gat.at[2:4, i, oy, :, c]
        return go(copy(a, a, pair(gc, d, 3), cpeer), copy(b, b, pair(gc, d, 4), cpeer))

    def neighbours(lower, upper, left, right, sem):
        to_right = copy(upper, left, pair(sem, 0), (dp, lax.rem(seq + 1, seqs)))
        to_left = copy(lower, right, pair(sem, 1), (dp, lax.rem(seq + seqs - 1, seqs)))
        return to_right, to_left

    def start_halo(halo):
        pl.when(seq < seqs - 1)(halo[0].start)
        pl.when(seq > 0)(halo[1].start)

    def wait_halo(halo):
        pl.when(seq > 0)(halo[0].wait_recv)
        pl.when(seq < seqs - 1)(halo[1].wait_recv)

    def wait_halo_sends(halo):
        pl.when(seq < seqs - 1)(halo[0].wait_send)
        pl.when(seq > 0)(halo[1].wait_send)

    tile = 32

    def activate_own():
        @pl.loop(0, rows // tile)
        def _(r):
            at_row = pl.multiple_of(r * tile, tile)
            value = in_ref[pl.ds(at_row, tile), :].astype(F32)
            act[pl.ds(pl.multiple_of(gap + at_row, tile), tile), :] = gelu_only(value).astype(BF16)

    def activate_halo():
        for side, start in ((0, 0), (1, gap + rows)):
            inside = (seq > 0) if side == 0 else (seq < seqs - 1)

            @pl.when(inside)
            def _():
                @pl.loop(0, gap // tile)
                def _(r):
                    at_row = pl.multiple_of(r * tile, tile)
                    value = xh[side, pl.ds(at_row, tile), :].astype(F32)
                    act[pl.ds(pl.multiple_of(start + at_row, tile), tile), :] = gelu_only(value).astype(BF16)

            @pl.when(jnp.logical_not(inside))
            def _():
                act[start:start + gap, :] = jnp.zeros((gap, chans), BF16)
                dpre[start:start + gap, :] = jnp.zeros((gap, hidden), BF16)

    def weight(k, i):
        return gat[k, i].reshape(cz, hidden)

    def multiply(d):
        i = at(d)
        for k in range(4):
            left = act[k * gap:k * gap + rows, columns(i)] if k < 3 else cot_ref[:, columns(i)]
            value = jnp.dot(left, weight(k, i), preferred_element_type=F32)
            if d == 0:
                acc[k] = value
            else:
                acc[k] += value

    first, second, cores = {}, {}, {}
    halo = neighbours(in_ref.at[0:gap], in_ref.at[gap:rows], xh.at[0], xh.at[1], hx)
    for t in range(planes + 3):
        if t < planes:
            if t > 0:
                arrived(zs[t])
            first[t], cores[t] = spread(t)
        if t == 0:
            load_in.wait()
            start_halo(halo)
            activate_own()
        if 0 <= t - 1 < planes:
            arrived(first[t - 1])
            second[t - 1], more = spread_again(t - 1)
            cores[t - 1] += more
        if 0 <= t - 2 < planes:
            arrived(second[t - 2])
            cores[t - 2] += share(t - 2)
        if t == 3:
            wait_halo(halo)
            activate_halo()
            load_cot.wait()
        if 0 <= t - 3 < planes:
            arrived(cores[t - 3])
            multiply(t - 3)

    @pl.loop(0, rows // tile)
    def _(r):
        here = pl.ds(pl.multiple_of(r * tile, tile), tile)
        pre = acc[0, here, :].astype(BF16).astype(F32)
        pre += acc[1, here, :].astype(BF16).astype(F32)
        pre += acc[2, here, :].astype(BF16).astype(F32)
        value, slope = gelu_and_slope(pre)
        mid[here, :] = value.astype(BF16)
        dpre[pl.ds(pl.multiple_of(gap + r * tile, tile), tile), :] = (acc[3, here, :] * slope).astype(BF16)

    halo_d = neighbours(
        dpre.at[gap:2 * gap], dpre.at[2 * gap:3 * gap],
        dpre.at[0:gap], dpre.at[gap + rows:2 * gap + rows], hd,
    )
    start_halo(halo_d)

    def to(d):
        return lax.rem(z + d, planes)

    def partial(n, d):
        for k in range(4):
            if k < 3:
                left, right = act[k * gap:k * gap + rows, columns(to(d))], dpre[gap:gap + rows, :]
            else:
                left, right = cot_ref[:, columns(to(d))], mid[...]
            value = lax.dot_general(left, right, (((0,), (0,)), ((), ())), preferred_element_type=F32)
            part[n, k] = value.reshape(part.shape[2:])
        sb0[n] = part[n, :, :, :, oc].astype(BF16)
        return go(copy(sb0.at[n], rb0.at[n], pair(q0, n), cpeer))

    def sum_cores(n, copies):
        arrived(copies)
        s0[n] = part[n, :, :, :, c] + rb0[n].astype(F32)
        sb1a[n] = s0[n, 0:2, :, ox].astype(BF16)
        sb1b[n] = s0[n, 2:4, oy].astype(BF16)
        return go(
            copy(sb1a.at[n], rb1a.at[n], pair(q1a, n), xpeer),
            copy(sb1b.at[n], rb1b.at[n], pair(q1b, n), ypeer),
        )

    def sum_first(n, copies):
        arrived(copies)
        s1a[n] = s0[n, 0:2, :, x] + rb1a[n].astype(F32)
        s1b[n] = s0[n, 2:4, y] + rb1b[n].astype(F32)
        sb2a[n] = s1a[n, :, oy].astype(BF16)
        sb2b[n] = s1b[n, :, ox].astype(BF16)
        return go(
            copy(sb2a.at[n], rb2a.at[n], pair(q2a, n), ypeer),
            copy(sb2b.at[n], rb2b.at[n], pair(q2b, n), xpeer),
        )

    def sum_second(n, d, copies):
        arrived(copies)
        s2[0:2] = s1a[n, :, y] + rb2a[n].astype(F32)
        s2[2:4] = s1b[n, :, x] + rb2b[n].astype(F32)
        if d == 0:
            return ()
        sb3[n] = s2[...].astype(BF16)
        return go(copy(sb3.at[n], rb3.at[n], pair(q3, n), zpeer(d)))

    def finish_columns(j):
        here = slice(j * cz, (j + 1) * cz)
        nt = (((1,), (1,)), ((), ()))
        total = lax.dot_general(dpre[2 * gap:4 * gap, :], weight(0, j), nt, preferred_element_type=F32)
        total += lax.dot_general(dpre[gap:3 * gap, :], weight(1, j), nt, preferred_element_type=F32)
        total += lax.dot_general(dpre[0:2 * gap, :], weight(2, j), nt, preferred_element_type=F32)
        dacc[0] = total
        dacc[1] = lax.dot_general(mid[...], weight(3, j), nt, preferred_element_type=F32)

        @pl.loop(0, rows // tile)
        def _(r):
            at_row = pl.ds(pl.multiple_of(r * tile, tile), tile)
            source = in_ref[at_row, here].astype(F32)
            out_ref[at_row, here] = (source + dacc[1, at_row, :]).astype(BF16)
            slope = gelu_and_slope(source)[1]
            ig_ref[at_row, here] = (cot_ref[at_row, here].astype(F32) + dacc[0, at_row, :] * slope).astype(BF16)

    order = list(range(1, planes)) + [0]
    r0, r1, r2, r3 = {}, {}, {}, []
    fills = list(range(planes))
    for t in range(planes + 4):
        if t < planes:
            r0[t] = partial(t, order[t])
        if 0 <= t - 1 < planes:
            r1[t - 1] = sum_cores(t - 1, r0[t - 1])
        if 0 <= t - 3 < planes:
            r2[t - 3] = sum_first(t - 3, r1[t - 3])
        if 0 <= t - 4 < planes:
            r3 += sum_second(t - 4, order[t - 4], r2[t - 4])
        if t >= 2 and fills:
            if t == 2:
                wait_halo(halo_d)
            finish_columns(fills.pop(0))
    for j in fills:
        finish_columns(j)
    arrived(r3)
    total = s2[...]
    for n in range(planes - 1):
        total += rb3[n].astype(F32)
    cg_ref[...] = total * factor

    for one in sends:
        one.wait_send()
    wait_halo_sends(halo)
    wait_halo_sends(halo_d)


def fused(planes, inputs, conv_weight, out_weight, cotangent):
    rows, chans = inputs.shape[1:]
    share, taps, hidden = conv_weight.shape
    factor = 1.0 / math.sqrt(rows * lax.axis_size("seq") * lax.axis_size("dp"))
    w = jnp.concatenate([conv_weight.transpose(1, 0, 2), out_weight[None]], axis=0)
    gap = rows // 2
    dma = pltpu.SemaphoreType.DMA
    blk = (share, hidden)
    cz = chans // planes
    vmem = pltpu.VMEM
    both = lambda shape: [vmem(shape, BF16), vmem(shape, BF16)]
    outputs, input_grad, grads = pl.pallas_call(
        functools.partial(block_kernel, planes, factor),
        out_shape=(
            jax.ShapeDtypeStruct((rows, chans), BF16),
            jax.ShapeDtypeStruct((rows, chans), BF16),
            jax.ShapeDtypeStruct((4,) + blk, F32),
        ),
        in_specs=[pl.BlockSpec(memory_space=pltpu.HBM)] * 2 + [pl.BlockSpec(memory_space=pltpu.VMEM)],
        out_specs=[pl.BlockSpec(memory_space=pltpu.VMEM)] * 3,
        scratch_shapes=[
            vmem((rows, chans), BF16),
            vmem((rows, chans), BF16),
            vmem((4, planes, 2, 2, 2) + blk, BF16),
            vmem((2, gap, chans), BF16),
            vmem((rows + 2 * gap, chans), BF16),
            vmem((4, rows, hidden), F32),
            vmem((rows, hidden), BF16),
            vmem((rows + 2 * gap, hidden), BF16),
            vmem((2, rows, cz), F32),
            vmem((planes, 4, 2, 2, 2) + blk, F32),
            vmem((planes, 4, 2, 2) + blk, F32),
            vmem((planes, 2, 2) + blk, F32),
            vmem((planes, 2, 2) + blk, F32),
            vmem((4,) + blk, F32),
            *both((planes, 4, 2, 2) + blk),
            *both((planes, 2, 2) + blk),
            *both((planes, 2, 2) + blk),
            *both((planes, 2) + blk),
            *both((planes, 2) + blk),
            *both((planes - 1, 4) + blk),
            dma((2, planes - 1)),
            dma((2, planes)),
            dma((2, planes)),
            dma((2, planes)),
            dma((2, planes)),
            dma((2, planes, 5)),
            dma((2, 2)),
            dma((2, 2)),
            dma((2, planes)),
            dma((2, planes)),
            dma((2, planes)),
            dma((2, planes)),
            dma((2, planes)),
            dma((2, planes - 1)),
            dma((3,)),
        ],
        compiler_params=pltpu.CompilerParams(
            collective_id=0, has_side_effects=True, vmem_limit_bytes=56 * 1024 * 1024
        ),
        cost_estimate=pl.CostEstimate(
            flops=2 * 12 * rows * chans * hidden, bytes_accessed=8 * rows * chans, transcendentals=0
        ),
    )(inputs[0], cotangent[0], w)
    return outputs[None], input_grad[None], grads[:3].transpose(1, 0, 2), grads[3]


def with_halo(cells, sides, width):
    for axis, dim in sides:
        count = lax.axis_size(axis)
        ends = count - 1
        head = lax.slice_in_dim(cells, 0, width, axis=dim)
        tail = lax.slice_in_dim(cells, cells.shape[dim] - width, cells.shape[dim], axis=dim)
        cells = jnp.concatenate(
            [
                lax.ppermute(tail, axis, [(i, (i + 1) % count) for i in range(ends)]),
                cells,
                lax.ppermute(head, axis, [((i + 1) % count, i) for i in range(ends)]),
            ],
            axis=dim,
        )
    return cells


def by_collectives(inputs, conv_weight, out_weight, cotangent):
    input_rows = inputs.shape[1]
    chans = inputs.shape[2]
    dilation_gap = input_rows // 2
    source = inputs[0]
    upstream = cotangent[0]
    wconv, wout = (
        lax.all_gather(conv_weight, ("dp", "seq"), axis=0, tiled=True),
        lax.all_gather(out_weight, ("dp", "seq"), axis=0, tiled=True),
    )
    hidden = wout.shape[1]
    wflat = wconv.reshape(chans, 3 * hidden)
    activated_value = jax.nn.gelu(source.astype(F32)).astype(BF16)
    widened_input = with_halo(activated_value, (("seq", 0),), dilation_gap)
    pre = jnp.zeros((input_rows, hidden), F32)
    for k in range(3):
        piece = jnp.dot(
            widened_input[k * dilation_gap : k * dilation_gap + input_rows],
            wconv[:, k, :],
            preferred_element_type=F32,
        )
        pre = pre + piece.astype(BF16).astype(F32)
    mid = jax.nn.gelu(pre).astype(BF16)
    outputs = (source.astype(F32) + jnp.dot(mid, wout.T, preferred_element_type=F32)).astype(BF16)
    dmid = jnp.dot(upstream, wout, preferred_element_type=F32)
    dpre = jax.vjp(jax.nn.gelu, pre)[1](dmid)[0].astype(BF16)
    wide = with_halo(dpre, (("seq", 0),), dilation_gap)
    shifted = jnp.concatenate(
        [wide[k * dilation_gap : k * dilation_gap + input_rows] for k in (2, 1, 0)], axis=1
    )
    dact = jnp.dot(shifted, wflat.T, preferred_element_type=F32)
    factor = 1.0 / math.sqrt(input_rows * lax.axis_size("seq") * lax.axis_size("dp"))
    conv_part = (
        jnp.einsum("pc,pk->ck", activated_value, shifted, preferred_element_type=F32) * factor
    ).reshape(chans, 3, hidden)
    out_part = jnp.einsum("pc,ph->ch", upstream, mid, preferred_element_type=F32) * factor
    input_grad = (
        upstream.astype(F32) + jax.vjp(jax.nn.gelu, source.astype(F32))[1](dact)[0]
    ).astype(BF16)
    conv_grad, out_grad = (
        lax.psum_scatter(conv_part, ("dp", "seq"), scatter_dimension=0, tiled=True),
        lax.psum_scatter(out_part, ("dp", "seq"), scatter_dimension=0, tiled=True),
    )
    return (outputs[None], input_grad[None], conv_grad, out_grad)


def solution(mesh):
    planes = mesh.shape["dp"] // 2

    def shards(inputs, conv_weight, out_weight, cotangent):
        aligned = conv_weight.shape[0] % 16 == 0 and mesh.shape["seq"] == 4 and 1 < planes <= 4
        if aligned:
            return fused(planes, inputs, conv_weight, out_weight, cotangent)
        return by_collectives(inputs, conv_weight, out_weight, cotangent)

    return jax.shard_map(
        shards,
        mesh=mesh,
        in_specs=(
            P("dp", "seq", None),
            P(("dp", "seq"), None, None),
            P(("dp", "seq"), None),
            P("dp", "seq", None),
        ),
        out_specs=(
            P("dp", "seq", None),
            P("dp", "seq", None),
            P(("dp", "seq"), None, None),
            P(("dp", "seq"), None),
        ),
        check_vma=False,
    )
```
